32 devices in a mesh: groups: 2 (over y), tm: 4 (over z), section: 2 (over x), head: 2 (over core).
Axes of the slice: x: 2, y: 2, z: 4, core: 2. Of those that a mesh axis runs over, the one named last changes fastest.
Arguments:
- latent: bfloat16 [4, 128, 5120], P(('groups', 'section'), 'tm', 'head'), parts along dimension 0, may hold values from -6 to 6
- head_weights: bfloat16 [2, 4, 40, 128, 128], P('section', None, 'head')
- modulation: float32 [2, 3, 5120], P('section', None, 'head'), may hold values from -3 to 3
- tile_mask: int32 [8, 2, 6], P(('groups', 'tm')), parts along dimension 0, may hold values from 0 to 1
- window: int32 [4], P('groups'), parts along dimension 0, may hold values from 1 to 3, as said below
Outputs:
- denoised: bfloat16 [4, 128, 5120], P(('groups', 'section'), 'tm', 'head'), parts along dimension 0
The draws below stay inside these ranges and needn't reach their ends.
There are 2 independent parts, one for each index of `groups`. The reference program is written for one: setup_inputs(seed, part) draws one part's arguments, and reference() takes and returns one part's arrays. A program takes and returns all parts, laid end to end along the dimension named above; an argument that names none is the same for every part. Nothing has to cross between parts.
Inputs may be any that keep to these rules, and one draw needn't show every extreme that they name: Some clip has a window of exactly 3 stretches.
All inputs are finite; a program needn't handle non-finite values.
Results may differ from the reference program's by a relative error of at most 0.0055.
Values may be sent and summed in bfloat16 or wider, within the bound.
A program may use at most 64 MiB of HBM per device.

```python
import math
import jax
import jax.numpy as jnp
from jax import lax

D = 5120
HEADS = 40
HD = 128
ROWS = 32
TILE = 16
SPAN = 3
TILES = 2
STRETCHES = 4
TOKENS = 128
CLIPS = 2
SECTIONS = 2


def draw_head_weights(key, part):
    shape = (SECTIONS, 4, HEADS, HD, HD)
    base = jax.random.normal(jax.random.fold_in(key, 11), shape, jnp.float32) * HD ** (-0.5)
    return base.astype(jnp.bfloat16)


def draw_tile_mask(key, part):
    level = jax.random.randint(jax.random.fold_in(key, 21), (STRETCHES, 1, 1), 15, 91)
    draws = jax.random.randint(jax.random.fold_in(key, 22), (STRETCHES, TILES, SPAN * TILES), 0, 100)
    return (draws < level).astype(jnp.int32)


def draw_window(key, part):
    lengths = jax.random.randint(jax.random.fold_in(key, 31), (CLIPS,), 1, SPAN + 1)
    picked = jax.random.randint(jax.random.fold_in(key, 32), (), 0, CLIPS)
    return jnp.where(jnp.arange(CLIPS) == picked, SPAN, lengths).astype(jnp.int32)


def block_levels(stream_key, shape, pieces, least, largest):
    loudness, own = 1.0, jax.random.fold_in(stream_key, 6)
    for position, parts in pieces:
        heights = jnp.exp(jax.random.uniform(jax.random.fold_in(own, position), (parts,), jnp.float32, least / len(pieces), largest / len(pieces)))
        loudness = loudness * jnp.repeat(heights, shape[position] // parts).reshape([-1 if axis == position else 1 for axis in range(len(shape))])
    return loudness


def scatter_about(key, extent, scale, most, pieces=(), kind=jnp.bfloat16):
    drawn = jax.random.normal(key, extent, jnp.float32) * scale
    if len(pieces) > 0:
        drawn = block_levels(key, extent, pieces, -0.22, 0.18) * drawn
    return jnp.clip(drawn, min=-most, max=most).astype(kind)


def setup_inputs(seed: int = 0, part: int = 0) -> dict:
    key_of = jax.random.split(jax.random.key(seed), 6)
    part_keys = jax.random.split(jax.random.fold_in(key_of[5], part), 6)
    return {
        "latent": scatter_about(part_keys[0], (CLIPS, TOKENS, D), 1.0, 6.0, ((0, 2), (1, 4), (2, 2))),
        "head_weights": draw_head_weights(jax.random.fold_in(key_of[5], 71), part),
        "modulation": scatter_about(key_of[2], (SECTIONS, 3, D), 0.5, 3.0, ((0, 2), (2, 2)), jnp.float32),
        "tile_mask": draw_tile_mask(jax.random.fold_in(jax.random.fold_in(key_of[5], part), 71), part),
        "window": draw_window(jax.random.fold_in(jax.random.fold_in(key_of[5], part), 71), part),
    }


epsilon = 1e-06

def allowed_mask(tile_mask, win_len):
    positions = jnp.arange(TOKENS)
    stretch_of = positions // ROWS
    tile_of = positions % ROWS // TILE
    distance = stretch_of[:, None] - stretch_of[None, :]
    column = jnp.clip((SPAN - 1 - distance) * TILES + tile_of[None, :], 0, SPAN * TILES - 1).astype(jnp.int32)
    marked = tile_mask[stretch_of[:, None], tile_of[:, None], column]
    own_tile = (distance == 0) & (tile_of[:, None] == tile_of[None, :])
    return (distance >= 0) & (distance < win_len) & (own_tile | (marked == 1))

def apply_layer(latent_rows, weights, modulate, allowed):
    values = latent_rows.astype(jnp.float32)
    mean_sq = lax.optimization_barrier(jnp.mean(values * values, axis=-1, keepdims=True))
    normed = (values * lax.rsqrt(mean_sq + epsilon) * (1.0 + modulate[1]) + modulate[0]).astype(jnp.bfloat16)
    heads_in = normed.reshape(TOKENS, HEADS, HD).astype(jnp.float32)
    projected = jnp.einsum('thd,mhde->mthe', heads_in, weights[:3].astype(jnp.float32)).astype(jnp.bfloat16)
    scores = jnp.einsum('qhd,khd->hqk', projected[0].astype(jnp.float32), projected[1].astype(jnp.float32)) * (1.0 / math.sqrt(HD))
    scores = jnp.where(allowed[None], scores, -1e+30)
    row_peak = lax.optimization_barrier(jnp.max(scores, axis=-1, keepdims=True))
    exponentials = jnp.exp(scores - row_peak)
    attn_probs = (exponentials / lax.optimization_barrier(jnp.sum(exponentials, axis=-1, keepdims=True))).astype(jnp.bfloat16)
    attended = jnp.einsum('hqk,khd->qhd', attn_probs.astype(jnp.float32), projected[2].astype(jnp.float32)).astype(jnp.bfloat16)
    mixed_out = jnp.einsum('qhd,hde->qhe', attended.astype(jnp.float32), weights[3].astype(jnp.float32)).reshape(TOKENS, D)
    return (values + modulate[2] * mixed_out).astype(jnp.bfloat16)

def reference(latent, head_weights, modulation, tile_mask, window):
    outputs = []
    for clip_index in range(CLIPS):
        allowed = allowed_mask(tile_mask, window[clip_index])
        clip_rows = latent[clip_index]
        for section in range(SECTIONS):
            clip_rows = apply_layer(clip_rows, head_weights[section], modulation[section], allowed)
        outputs.append(clip_rows)
    return jnp.stack(outputs)
```

```python
import functools
import math

import jax
import jax.numpy as jnp
from jax import lax
from jax.experimental import pallas as pl
from jax.experimental.pallas import tpu as pltpu
from jax.sharding import PartitionSpec as P

D = 5120


epsilon = 1e-06
MESH_IDS = pl.DeviceIdType.MESH


def from_behind(block, axis, distance):
    devices = range(lax.axis_size(axis))
    route = [(i - distance, i) for i in devices if i - distance in devices]
    return lax.ppermute(block, axis, route)


def passed_along(block, axis, distance):
    devices = range(lax.axis_size(axis))
    route = [((i - distance) % len(devices), i) for i in devices]
    return lax.ppermute(block, axis, route)


def ring_shards(latent, head_weights, modulation, tile_mask, window):
    section_count = lax.axis_size("section")
    my_section = lax.axis_index("section")
    my_stretch = lax.axis_index("tm")
    row_count = latent.shape[1]
    feature_count = latent.shape[2]
    weights = head_weights[0]
    head_count = weights.shape[1]
    head_size = weights.shape[2]
    modulate = modulation[0]
    tile_marks = tile_mask[0]
    tile_count = tile_marks.shape[0]
    span_count = tile_marks.shape[1] // tile_count
    tile_rows = row_count // tile_count
    scale_factor = 1.0 / math.sqrt(head_size)
    expanded = jnp.repeat(jnp.repeat(tile_marks, tile_rows, axis=0), tile_rows, axis=1) == 1
    query_tile = jnp.arange(row_count) // tile_rows
    key_index = jnp.arange(span_count * row_count)
    key_dist = span_count - 1 - key_index // row_count
    key_tile = key_index % row_count // tile_rows
    own_tile = (key_dist == 0)[None, :] & (query_tile[:, None] == key_tile[None, :])
    fixed_mask = expanded | own_tile
    reachable = my_stretch - key_dist >= 0

    def tick_body(tick_index, current):
        clip_index = (my_section - tick_index) % section_count
        active = tick_index == my_section + (section_count - clip_index) % section_count
        win_len = window[clip_index]
        allowed = fixed_mask & (reachable & (key_dist < win_len))[None, :]
        values = current.astype(jnp.float32)
        square_sum = lax.psum(jnp.sum(values * values, axis=-1), "head")
        mean_sq = (square_sum / D)[:, None]
        normed = (values * lax.rsqrt(mean_sq + epsilon) * (1.0 + modulate[1]) + modulate[0]).astype(
            jnp.bfloat16
        )
        heads_in = normed.reshape(row_count, head_count, head_size)
        projected = jnp.einsum(
            "rhd,mhde->mrhe", heads_in, weights[:3], preferred_element_type=jnp.float32
        ).astype(jnp.bfloat16)
        key_value = projected[1:].reshape(2, row_count, feature_count)
        earlier = []
        passed = key_value
        for offset in range(1, span_count):
            passed = from_behind(passed, "tm", 1)
            earlier.append(passed)
        window_keys = jnp.concatenate(earlier[::-1] + [key_value], axis=1)
        window_keys = window_keys.reshape(2, span_count * row_count, head_count, head_size)
        scores = (
            jnp.einsum(
                "qhd,khd->hqk", projected[0], window_keys[0], preferred_element_type=jnp.float32
            )
            * scale_factor
        )
        scores = jnp.where(allowed[None], scores, -1e30)
        row_peak = jnp.max(scores, axis=-1, keepdims=True)
        exponentials = jnp.exp(scores - row_peak)
        attn_probs = (exponentials / jnp.sum(exponentials, axis=-1, keepdims=True)).astype(
            jnp.bfloat16
        )
        attended = jnp.einsum(
            "hqk,khd->qhd", attn_probs, window_keys[1], preferred_element_type=jnp.float32
        ).astype(jnp.bfloat16)
        mixed_out = jnp.einsum(
            "qhd,hde->qhe", attended, weights[3], preferred_element_type=jnp.float32
        ).reshape(row_count, feature_count)
        updated = (values + modulate[2] * mixed_out).astype(jnp.bfloat16)
        current = jnp.where(active, updated, current)
        return passed_along(current, "section", 1)

    finished = lax.fori_loop(0, 2 * section_count, tick_body, latent[0])
    return finished[None]


def rollout_kernel(
    stretches, cores,
    marks_ref, window_ref, latent_ref, weights_ref, modulation_ref,
    out_ref,
    xin, xmid, stage, marks, held, mods, squares,
    in_send, in_recv, mark_send, mark_recv, own_sem, mod_sem, modx_sem,
    local_sem, x_send, x_recv, y_send, y_recv,
    sq_send, sq_recv, out_send, out_recv, out_own,
):
    g = lax.axis_index("groups")
    t = lax.axis_index("tm")
    s = lax.axis_index("section")
    h = lax.axis_index("head")
    heads = held.shape[2]
    size = held.shape[3]
    rows = xin.shape[1]
    width = heads * size
    tokens = stretches * rows
    tiles = marks_ref.shape[1]
    columns = marks_ref.shape[2]
    span = columns // tiles
    scale = 1.0 / math.sqrt(size)
    other_s = 1 - s
    other_g = 1 - g

    peers = [
        (dt, dh, lax.rem(t + dt, stretches), lax.rem(h + dh, cores))
        for dt in range(stretches) for dh in range(cores) if (dt, dh) != (0, 0)
    ]

    def lanes(stretch):
        return pl.ds(pl.multiple_of(stretch * width, size), width)

    def remote(src, dst, send, recv, **where):
        return pltpu.make_async_remote_copy(
            src_ref=src, dst_ref=dst, send_sem=send, recv_sem=recv,
            device_id=where, device_id_type=MESH_IDS,
        )

    barrier = pltpu.get_barrier_semaphore()
    for dt, dh, pt, ph in peers:
        pl.semaphore_signal(barrier, inc=1, device_id={"tm": pt, "head": ph}, device_id_type=MESH_IDS)
    pl.semaphore_signal(barrier, inc=1, device_id={"section": other_s}, device_id_type=MESH_IDS)
    pl.semaphore_signal(barrier, inc=1, device_id={"groups": other_g}, device_id_type=MESH_IDS)

    own_copy = pltpu.make_async_copy(latent_ref.at[0, :, lanes(t)], xin.at[t], own_sem)
    own_copy.start()
    mod_copy = pltpu.make_async_copy(modulation_ref.at[0, :, lanes(t)], mods.at[s], mod_sem)
    mod_copy.start()
    local = []
    for j in range(heads):
        copy = pltpu.make_async_copy(
            weights_ref.at[0, :, t * heads + j], held.at[s, :, j], local_sem.at[j]
        )
        copy.start()
        local.append(copy)

    row = lax.broadcasted_iota(jnp.int32, (rows, tokens), 0)
    key = lax.broadcasted_iota(jnp.int32, (rows, tokens), 1)
    tile_rows = rows // tiles
    row_tile = row // tile_rows
    key_tile = key % rows // tile_rows
    distance = t - key // rows
    column = (span - 1 - distance) * tiles + key_tile
    marked = jnp.zeros((rows, tokens), jnp.int32)
    for a in range(tiles):
        for c in range(columns):
            marked = jnp.where((row_tile == a) & (column == c), marks_ref[0, a, c], marked)
    own_tile = (distance == 0) & (row_tile == key_tile)
    seen = (distance >= 0) & (distance < window_ref[s]) & (own_tile | (marked == 1))
    marks[t] = jnp.where(seen, 1.0, 0.0).astype(jnp.bfloat16)

    pl.semaphore_wait(barrier, len(peers) + 2)

    half = pl.ds(2 * g, 2)
    other_half = pl.ds(2 * other_g, 2)
    mod_remote = remote(
        modulation_ref.at[0, :, lanes(t)], mods.at[s], modx_sem.at[0], modx_sem.at[1], section=other_s
    )
    x_copies = [
        remote(
            weights_ref.at[0, half, t * heads + j], held.at[s, half, j],
            x_send.at[j], x_recv.at[j], section=other_s,
        )
        for j in range(heads)
    ]
    y_copies = [
        remote(
            held.at[other_s, half, j], held.at[other_s, half, j],
            y_send.at[j], y_recv.at[j], groups=other_g,
        )
        for j in range(heads)
    ]
    in_copies, mark_copies = [], []
    for dt in range(1, stretches):
        pt = lax.rem(t + dt, stretches)
        in_copies.append(
            remote(latent_ref.at[0, :, lanes(pt)], xin.at[t], in_send.at[dt], in_recv.at[dt], tm=pt)
        )
        mark_copies.append(
            remote(marks.at[t], marks.at[t], mark_send.at[dt], mark_recv.at[dt], tm=pt)
        )
    x_copies[0].start()
    for copy in in_copies:
        copy.start()
    mod_remote.start()
    for copy in x_copies[1:]:
        copy.start()
    for copy in mark_copies:
        copy.start()

    def forward(j):
        remote(
            weights_ref.at[0, half, t * heads + j], held.at[other_s, half, j],
            x_send.at[j], x_recv.at[j], section=other_s,
        ).wait_recv()
        y_copies[j].start()

    def wait_forwarded(j):
        remote(
            held.at[other_s, half, j], held.at[other_s, other_half, j],
            y_send.at[j], y_recv.at[j], groups=other_g,
        ).wait_recv()

    slot = t * cores + h

    def square_copies(layer):
        return [
            remote(
                squares.at[layer, slot], squares.at[layer, slot],
                sq_send.at[layer, dt * cores + dh], sq_recv.at[layer, dt * cores + dh],
                tm=pt, head=ph,
            )
            for dt, dh, pt, ph in peers
        ]

    def share_squares(layer, total):
        turned = total.T
        squares[layer, slot] = jnp.sum(turned.reshape(size // 8, 8, tokens), axis=0)
        for copy in square_copies(layer):
            copy.start()

    def row_scale(layer):
        for dt, dh, pt, ph in peers:
            st = lax.rem(t - dt + stretches, stretches)
            sh = lax.rem(h - dh + cores, cores)
            source = st * cores + sh
            remote(
                squares.at[layer, slot], squares.at[layer, source],
                sq_send.at[layer, dt * cores + dh], sq_recv.at[layer, dt * cores + dh],
                tm=pt, head=ph,
            ).wait_recv()
        total = jnp.sum(jnp.sum(squares[layer], axis=0), axis=0, keepdims=True)
        inverse = lax.rsqrt(total / D + epsilon)
        return jnp.broadcast_to(inverse, (size, tokens)).T

    def block_of(ref, j):
        return ref[:, :, j * size : (j + 1) * size].reshape(tokens, size)

    def one_head(layer, j, values, inverse, allowed):
        modulate = mods[layer, :, j * size : (j + 1) * size]
        normed = (values * inverse * (1.0 + modulate[1:2]) + modulate[0:1]).astype(jnp.bfloat16)
        q, k, v = (
            jnp.dot(normed, held[layer, m, j], preferred_element_type=jnp.float32).astype(jnp.bfloat16)
            for m in range(3)
        )
        scores = lax.dot_general(
            q, k, (((1,), (1,)), ((), ())), preferred_element_type=jnp.float32
        ) * scale
        scores = jnp.where(allowed, scores, -1e30)
        weight = jnp.exp(scores - jnp.max(scores, axis=-1, keepdims=True))
        probs = (weight / jnp.sum(weight, axis=-1, keepdims=True)).astype(jnp.bfloat16)
        attended = jnp.dot(probs, v, preferred_element_type=jnp.float32).astype(jnp.bfloat16)
        mixed = jnp.dot(attended, held[layer, 3, j], preferred_element_type=jnp.float32)
        return (values + modulate[2:3] * mixed).astype(jnp.bfloat16)

    own_copy.wait()
    for dt in range(1, stretches):
        st = lax.rem(t - dt + stretches, stretches)
        remote(
            latent_ref.at[0, :, lanes(t)], xin.at[st], in_send.at[dt], in_recv.at[dt], tm=st
        ).wait_recv()
    total = jnp.zeros((tokens, size), jnp.float32)
    for j in range(heads):
        values = block_of(xin, j).astype(jnp.float32)
        total += values * values
    share_squares(0, total)

    for dt in range(1, stretches):
        st = lax.rem(t - dt + stretches, stretches)
        remote(marks.at[t], marks.at[st], mark_send.at[dt], mark_recv.at[dt], tm=st).wait_recv()
    mod_copy.wait()
    remote(
        modulation_ref.at[0, :, lanes(t)], mods.at[other_s], modx_sem.at[0], modx_sem.at[1], section=other_s
    ).wait_recv()
    allowed = marks[...].reshape(tokens, tokens).astype(jnp.float32) > 0.5

    inverse = row_scale(0)
    forward(0)
    total = jnp.zeros((tokens, size), jnp.float32)
    for j in range(heads):
        if j + 1 < heads:
            forward(j + 1)

        @pl.when(s == 0)
        def _():
            local[j].wait()

        @pl.when(s == 1)
        def _():
            wait_forwarded(j)

        result = one_head(0, j, block_of(xin, j).astype(jnp.float32), inverse, allowed)
        xmid[j] = result
        rounded = result.astype(jnp.float32)
        total += rounded * rounded
    share_squares(1, total)

    @pl.when(s == 0)
    def _():
        for j in range(heads):
            wait_forwarded(j)

    @pl.when(s == 1)
    def _():
        for j in range(heads):
            local[j].wait()

    inverse = row_scale(1)
    finals = []
    for j in range(heads):
        result = one_head(1, j, xmid[j].astype(jnp.float32), inverse, allowed)
        stage[j] = result.reshape(stretches, rows, size)
        place = pl.ds(pl.multiple_of((t * heads + j) * size, size), size)
        for dt in range(1, stretches):
            pt = lax.rem(t + dt, stretches)
            copy = remote(
                stage.at[j, pt], out_ref.at[0, :, place], out_send.at[j, dt], out_recv.at[j, dt], tm=pt
            )
            copy.start()
            finals.append(copy)
        copy = pltpu.make_async_copy(stage.at[j, t], out_ref.at[0, :, place], out_own.at[j])
        copy.start()
        finals.append(copy)

    for copy in in_copies + mark_copies + [mod_remote] + x_copies + y_copies:
        copy.wait_send()
    for layer in range(2):
        for copy in square_copies(layer):
            copy.wait_send()
    for j in range(heads):
        for dt in range(1, stretches):
            st = lax.rem(t - dt + stretches, stretches)
            place = pl.ds(pl.multiple_of((st * heads + j) * size, size), size)
            remote(
                stage.at[j, t], out_ref.at[0, :, place], out_send.at[j, dt], out_recv.at[j, dt], tm=st
            ).wait()
        pltpu.make_async_copy(
            stage.at[j, t],
            out_ref.at[0, :, pl.ds(pl.multiple_of((t * heads + j) * size, size), size)],
            out_own.at[j],
        ).wait()


def gathered_shards(latent, head_weights, modulation, tile_mask, window):
    stretches = lax.axis_size("tm")
    cores = lax.axis_size("head")
    rows, features = latent.shape[1:]
    maps, head_count, size = head_weights.shape[1:4]
    heads = head_count // stretches
    width = heads * size
    tokens = stretches * rows
    partners = stretches * cores
    dma = pltpu.SemaphoreType.DMA
    flops = 2 * heads * 6 * 2 * tokens * size * size
    return pl.pallas_call(
        functools.partial(rollout_kernel, stretches, cores),
        out_shape=jax.ShapeDtypeStruct(latent.shape, latent.dtype),
        in_specs=[pl.BlockSpec(memory_space=pltpu.SMEM)] * 2 + [pl.BlockSpec(memory_space=pl.ANY)] * 3,
        out_specs=pl.BlockSpec(memory_space=pl.ANY),
        scratch_shapes=[
            pltpu.VMEM((stretches, rows, width), jnp.bfloat16),
            pltpu.VMEM((heads, tokens, size), jnp.bfloat16),
            pltpu.VMEM((heads, stretches, rows, size), jnp.bfloat16),
            pltpu.VMEM((stretches, rows, tokens), jnp.bfloat16),
            pltpu.VMEM((2, maps, heads, size, size), jnp.bfloat16),
            pltpu.VMEM((2, modulation.shape[1], width), jnp.float32),
            pltpu.VMEM((2, partners, 8, tokens), jnp.float32),
            dma((stretches,)), dma((stretches,)), dma((stretches,)), dma((stretches,)),
            dma, dma, dma((2,)),
            dma((heads,)), dma((heads,)), dma((heads,)), dma((heads,)), dma((heads,)),
            dma((2, partners)), dma((2, partners)),
            dma((heads, stretches)), dma((heads, stretches)), dma((heads,)),
        ],
        compiler_params=pltpu.CompilerParams(
            collective_id=0, has_side_effects=True, vmem_limit_bytes=56 * 2**20
        ),
        cost_estimate=pl.CostEstimate(flops=flops, bytes_accessed=4 * 2**20, transcendentals=0),
    )(tile_mask, window, latent, head_weights, modulation)


def solution(mesh):
    sizes = dict(mesh.shape)

    def shards(latent, head_weights, *rest):
        pairs = sizes["section"] == 2 and sizes["groups"] == 2 and head_weights.shape[1] == 4
        even = head_weights.shape[2] % sizes["tm"] == 0
        chosen = gathered_shards if pairs and even else ring_shards
        return chosen(latent, head_weights, *rest)

    return jax.shard_map(
        shards,
        mesh=mesh,
        in_specs=(
            P(("groups", "section"), "tm", "head"),
            P("section", None, "head", None, None),
            P("section", None, "head"),
            P(("groups", "tm"), None, None),
            P("groups"),
        ),
        out_specs=P(("groups", "section"), "tm", "head"),
        check_vma=False,
    )
```

```python
import functools
import math

import jax
import jax.numpy as jnp
from jax import lax
from jax.experimental import pallas as pl
from jax.experimental.pallas import tpu as pltpu
from jax.sharding import PartitionSpec as P

D = 5120


epsilon = 1e-06
MESH_IDS = pl.DeviceIdType.MESH


def from_behind(block, axis, distance):
    devices = range(lax.axis_size(axis))
    route = [(i - distance, i) for i in devices if i - distance in devices]
    return lax.ppermute(block, axis, route)


def passed_along(block, axis, distance):
    devices = range(lax.axis_size(axis))
    route = [((i - distance) % len(devices), i) for i in devices]
    return lax.ppermute(block, axis, route)


def ring_shards(latent, head_weights, modulation, tile_mask, window):
    section_count = lax.axis_size("section")
    my_section = lax.axis_index("section")
    my_stretch = lax.axis_index("tm")
    row_count = latent.shape[1]
    feature_count = latent.shape[2]
    weights = head_weights[0]
    head_count = weights.shape[1]
    head_size = weights.shape[2]
    modulate = modulation[0]
    tile_marks = tile_mask[0]
    tile_count = tile_marks.shape[0]
    span_count = tile_marks.shape[1] // tile_count
    tile_rows = row_count // tile_count
    scale_factor = 1.0 / math.sqrt(head_size)
    expanded = jnp.repeat(jnp.repeat(tile_marks, tile_rows, axis=0), tile_rows, axis=1) == 1
    query_tile = jnp.arange(row_count) // tile_rows
    key_index = jnp.arange(span_count * row_count)
    key_dist = span_count - 1 - key_index // row_count
    key_tile = key_index % row_count // tile_rows
    own_tile = (key_dist == 0)[None, :] & (query_tile[:, None] == key_tile[None, :])
    fixed_mask = expanded | own_tile
    reachable = my_stretch - key_dist >= 0

    def tick_body(tick_index, current):
        clip_index = (my_section - tick_index) % section_count
        active = tick_index == my_section + (section_count - clip_index) % section_count
        win_len = window[clip_index]
        allowed = fixed_mask & (reachable & (key_dist < win_len))[None, :]
        values = current.astype(jnp.float32)
        square_sum = lax.psum(jnp.sum(values * values, axis=-1), "head")
        mean_sq = (square_sum / D)[:, None]
        normed = (values * lax.rsqrt(mean_sq + epsilon) * (1.0 + modulate[1]) + modulate[0]).astype(
            jnp.bfloat16
        )
        heads_in = normed.reshape(row_count, head_count, head_size)
        projected = jnp.einsum(
            "rhd,mhde->mrhe", heads_in, weights[:3], preferred_element_type=jnp.float32
        ).astype(jnp.bfloat16)
        key_value = projected[1:].reshape(2, row_count, feature_count)
        earlier = []
        passed = key_value
        for offset in range(1, span_count):
            passed = from_behind(passed, "tm", 1)
            earlier.append(passed)
        window_keys = jnp.concatenate(earlier[::-1] + [key_value], axis=1)
        window_keys = window_keys.reshape(2, span_count * row_count, head_count, head_size)
        scores = (
            jnp.einsum(
                "qhd,khd->hqk", projected[0], window_keys[0], preferred_element_type=jnp.float32
            )
            * scale_factor
        )
        scores = jnp.where(allowed[None], scores, -1e30)
        row_peak = jnp.max(scores, axis=-1, keepdims=True)
        exponentials = jnp.exp(scores - row_peak)
        attn_probs = (exponentials / jnp.sum(exponentials, axis=-1, keepdims=True)).astype(
            jnp.bfloat16
        )
        attended = jnp.einsum(
            "hqk,khd->qhd", attn_probs, window_keys[1], preferred_element_type=jnp.float32
        ).astype(jnp.bfloat16)
        mixed_out = jnp.einsum(
            "qhd,hde->qhe", attended, weights[3], preferred_element_type=jnp.float32
        ).reshape(row_count, feature_count)
        updated = (values + modulate[2] * mixed_out).astype(jnp.bfloat16)
        current = jnp.where(active, updated, current)
        return passed_along(current, "section", 1)

    finished = lax.fori_loop(0, 2 * section_count, tick_body, latent[0])
    return finished[None]


def rollout_kernel(
    stretches, cores,
    marks_ref, window_ref, latent_ref, weights_ref, modulation_ref,
    out_ref,
    mine, xin, xmid, stage, marks, held, mods, squares,
    in_send, in_recv, mark_send, mark_recv, mine_sem, own_sem, mod_sem, modx_sem,
    local_sem, x_send, x_recv, y_send, y_recv,
    sq_send, sq_recv, out_send, out_recv, out_own,
):
    g = lax.axis_index("groups")
    t = lax.axis_index("tm")
    s = lax.axis_index("section")
    h = lax.axis_index("head")
    heads = held.shape[2]
    size = held.shape[3]
    rows = xin.shape[1]
    width = heads * size
    tokens = stretches * rows
    tiles = marks_ref.shape[1]
    columns = marks_ref.shape[2]
    span = columns // tiles
    scale = 1.0 / math.sqrt(size)
    other_s = 1 - s
    other_g = 1 - g

    peers = [
        (dt, dh, lax.rem(t + dt, stretches), lax.rem(h + dh, cores))
        for dt in range(stretches) for dh in range(cores) if (dt, dh) != (0, 0)
    ]

    def lanes(stretch):
        return pl.ds(pl.multiple_of(stretch * width, size), width)

    def remote(src, dst, send, recv, **where):
        return pltpu.make_async_remote_copy(
            src_ref=src, dst_ref=dst, send_sem=send, recv_sem=recv,
            device_id=where, device_id_type=MESH_IDS,
        )

    barrier = pltpu.get_barrier_semaphore()
    for dt, dh, pt, ph in peers:
        pl.semaphore_signal(barrier, inc=1, device_id={"tm": pt, "head": ph}, device_id_type=MESH_IDS)
    pl.semaphore_signal(barrier, inc=1, device_id={"section": other_s}, device_id_type=MESH_IDS)
    pl.semaphore_signal(barrier, inc=1, device_id={"groups": other_g}, device_id_type=MESH_IDS)

    mine_copy = pltpu.make_async_copy(latent_ref.at[0], mine, mine_sem)
    mine_copy.start()
    own_copy = pltpu.make_async_copy(latent_ref.at[0, :, lanes(t)], xin.at[t], own_sem)
    own_copy.start()
    mod_copy = pltpu.make_async_copy(modulation_ref.at[:, :, lanes(t)], mods.at[s], mod_sem)
    mod_copy.start()
    local = []
    for j in range(heads):
        copy = pltpu.make_async_copy(
            weights_ref.at[0, :, t * heads + j], held.at[s, :, j], local_sem.at[j]
        )
        copy.start()
        local.append(copy)

    row = lax.broadcasted_iota(jnp.int32, (rows, tokens), 0)
    key = lax.broadcasted_iota(jnp.int32, (rows, tokens), 1)
    tile_rows = rows // tiles
    row_tile = row // tile_rows
    key_tile = key % rows // tile_rows
    distance = t - key // rows
    column = (span - 1 - distance) * tiles + key_tile
    marked = jnp.zeros((rows, tokens), jnp.int32)
    for a in range(tiles):
        for c in range(columns):
            marked = jnp.where((row_tile == a) & (column == c), marks_ref[0, a, c], marked)
    own_tile = (distance == 0) & (row_tile == key_tile)
    seen = (distance >= 0) & (distance < window_ref[s]) & (own_tile | (marked == 1))
    marks[t] = jnp.where(seen, 1.0, 0.0).astype(jnp.bfloat16)

    slot = t * cores + h

    def square_copies(layer):
        return [
            remote(
                squares.at[layer, slot], squares.at[layer, slot],
                sq_send.at[layer, dt * cores + dh], sq_recv.at[layer, dt * cores + dh],
                tm=pt, head=ph,
            )
            for dt, dh, pt, ph in peers
        ]

    def put_squares(layer, total):
        turned = total.T
        squares[layer, slot] = jnp.sum(turned.reshape(size // 8, 8, tokens), axis=0)

    mine_copy.wait()
    total = jnp.zeros((rows, size), jnp.float32)
    for j in range(stretches * heads):
        values = mine[:, j * size : (j + 1) * size].astype(jnp.float32)
        total += values * values
    put_squares(0, jnp.concatenate([total] * stretches, axis=0))

    pl.semaphore_wait(barrier, len(peers) + 2)

    half = pl.ds(2 * g, 2)
    other_half = pl.ds(2 * other_g, 2)
    mod_remote = remote(
        modulation_ref.at[:, :, lanes(t)], mods.at[s], modx_sem.at[0], modx_sem.at[1], section=other_s
    )
    x_copies = [
        remote(
            weights_ref.at[0, half, t * heads + j], held.at[s, half, j],
            x_send.at[j], x_recv.at[j], section=other_s,
        )
        for j in range(heads)
    ]
    y_copies = [
        remote(
            held.at[other_s, half, j], held.at[other_s, half, j],
            y_send.at[j], y_recv.at[j], groups=other_g,
        )
        for j in range(heads)
    ]
    in_copies, mark_copies = [], []
    for dt in range(1, stretches):
        pt = lax.rem(t + dt, stretches)
        in_copies.append(
            remote(latent_ref.at[0, :, lanes(pt)], xin.at[t], in_send.at[dt], in_recv.at[dt], tm=pt)
        )
        mark_copies.append(
            remote(marks.at[t], marks.at[t], mark_send.at[dt], mark_recv.at[dt], tm=pt)
        )
    first_squares = square_copies(0)
    for copy in x_copies[:2] + in_copies + first_squares + x_copies[2:] + [mod_remote]:
        copy.start()
    for copy in mark_copies:
        copy.start()

    def forward(j):
        remote(
            weights_ref.at[0, half, t * heads + j], held.at[other_s, half, j],
            x_send.at[j], x_recv.at[j], section=other_s,
        ).wait_recv()
        y_copies[j].start()

    def wait_forwarded(j):
        remote(
            held.at[other_s, half, j], held.at[other_s, other_half, j],
            y_send.at[j], y_recv.at[j], groups=other_g,
        ).wait_recv()

    def row_scale(layer):
        for dt, dh, pt, ph in peers:
            st = lax.rem(t - dt + stretches, stretches)
            sh = lax.rem(h - dh + cores, cores)
            source = st * cores + sh
            remote(
                squares.at[layer, slot], squares.at[layer, source],
                sq_send.at[layer, dt * cores + dh], sq_recv.at[layer, dt * cores + dh],
                tm=pt, head=ph,
            ).wait_recv()
        if layer == 0:
            stretch = lax.broadcasted_iota(jnp.int32, (8, tokens), 1) // rows
            total = jnp.zeros((8, tokens), jnp.float32)
            for source in range(stretches * cores):
                total += jnp.where(stretch == source // cores, squares[0, source], 0.0)
        else:
            total = jnp.sum(squares[layer], axis=0)
        total = jnp.sum(total, axis=0, keepdims=True)
        inverse = lax.rsqrt(total / D + epsilon)
        return jnp.broadcast_to(inverse, (size, tokens)).T

    def block_of(ref, j):
        return ref[:, :, j * size : (j + 1) * size].reshape(tokens, size)

    def some_heads(layer, numbers, inputs, inverse, allowed):
        modulate = [mods[layer, :, 0, j * size : (j + 1) * size] for j in numbers]
        normed = [
            (x * inverse * (1.0 + m[1:2]) + m[0:1]).astype(jnp.bfloat16)
            for x, m in zip(inputs, modulate)
        ]
        q, k, v = (
            [
                jnp.dot(n, held[layer, m, j], preferred_element_type=jnp.float32).astype(jnp.bfloat16)
                for j, n in zip(numbers, normed)
            ]
            for m in range(3)
        )
        scores = [
            lax.dot_general(a, b, (((1,), (1,)), ((), ())), preferred_element_type=jnp.float32) * scale
            for a, b in zip(q, k)
        ]
        scores = [jnp.where(allowed, x, -1e30) for x in scores]
        weight = [jnp.exp(x - jnp.max(x, axis=-1, keepdims=True)) for x in scores]
        probs = [(x / jnp.sum(x, axis=-1, keepdims=True)).astype(jnp.bfloat16) for x in weight]
        attended = [
            jnp.dot(p, b, preferred_element_type=jnp.float32).astype(jnp.bfloat16)
            for p, b in zip(probs, v)
        ]
        mixed = [
            jnp.dot(a, held[layer, 3, j], preferred_element_type=jnp.float32)
            for j, a in zip(numbers, attended)
        ]
        return [
            (x + m[2:3] * y).astype(jnp.bfloat16) for x, m, y in zip(inputs, modulate, mixed)
        ]

    def ahead(j):
        if j < heads:
            forward(j)

    ahead(0)
    ahead(1)
    own_copy.wait()
    for dt in range(1, stretches):
        st = lax.rem(t - dt + stretches, stretches)
        remote(
            latent_ref.at[0, :, lanes(t)], xin.at[st], in_send.at[dt], in_recv.at[dt], tm=st
        ).wait_recv()
    ahead(2)

    for dt in range(1, stretches):
        st = lax.rem(t - dt + stretches, stretches)
        remote(marks.at[t], marks.at[st], mark_send.at[dt], mark_recv.at[dt], tm=st).wait_recv()
    mod_copy.wait()
    remote(
        modulation_ref.at[:, :, lanes(t)], mods.at[other_s], modx_sem.at[0], modx_sem.at[1], section=other_s
    ).wait_recv()
    allowed = marks[...].reshape(tokens, tokens).astype(jnp.float32) > 0.5

    inverse = row_scale(0)
    ahead(3)
    total = jnp.zeros((tokens, size), jnp.float32)
    for j in range(heads):
        ahead(j + 4)

        @pl.when(s == 0)
        def _():
            local[j].wait()

        @pl.when(s == 1)
        def _():
            wait_forwarded(j)

        (result,) = some_heads(0, [j], [block_of(xin, j).astype(jnp.float32)], inverse, allowed)
        xmid[j] = result
        rounded = result.astype(jnp.float32)
        total += rounded * rounded
    put_squares(1, total)
    for copy in square_copies(1):
        copy.start()

    @pl.when(s == 0)
    def _():
        for j in range(heads):
            wait_forwarded(j)

    @pl.when(s == 1)
    def _():
        for j in range(heads):
            local[j].wait()

    inverse = row_scale(1)
    finals = []
    numbers = list(range(heads))
    inputs = [xmid[j].astype(jnp.float32) for j in numbers]
    for j, result in enumerate(some_heads(1, numbers, inputs, inverse, allowed)):
        stage[j] = result.reshape(stretches, rows, size)
        place = pl.ds(pl.multiple_of((t * heads + j) * size, size), size)
        for dt in range(1, stretches):
            pt = lax.rem(t + dt, stretches)
            copy = remote(
                stage.at[j, pt], out_ref.at[0, :, place], out_send.at[j, dt], out_recv.at[j, dt], tm=pt
            )
            copy.start()
            finals.append(copy)
        copy = pltpu.make_async_copy(stage.at[j, t], out_ref.at[0, :, place], out_own.at[j])
        copy.start()
        finals.append(copy)

    for copy in in_copies + mark_copies + [mod_remote] + x_copies + y_copies:
        copy.wait_send()
    for layer in range(2):
        for copy in square_copies(layer):
            copy.wait_send()
    for j in range(heads):
        for dt in range(1, stretches):
            st = lax.rem(t - dt + stretches, stretches)
            place = pl.ds(pl.multiple_of((st * heads + j) * size, size), size)
            remote(
                stage.at[j, t], out_ref.at[0, :, place], out_send.at[j, dt], out_recv.at[j, dt], tm=st
            ).wait()
        pltpu.make_async_copy(
            stage.at[j, t],
            out_ref.at[0, :, pl.ds(pl.multiple_of((t * heads + j) * size, size), size)],
            out_own.at[j],
        ).wait()


def gathered_shards(latent, head_weights, modulation, tile_mask, window):
    stretches = lax.axis_size("tm")
    cores = lax.axis_size("head")
    rows, features = latent.shape[1:]
    maps, head_count, size = head_weights.shape[1:4]
    heads = head_count // stretches
    width = heads * size
    tokens = stretches * rows
    partners = stretches * cores
    dma = pltpu.SemaphoreType.DMA
    flops = 2 * heads * 6 * 2 * tokens * size * size
    return pl.pallas_call(
        functools.partial(rollout_kernel, stretches, cores),
        out_shape=jax.ShapeDtypeStruct(latent.shape, latent.dtype),
        in_specs=[pl.BlockSpec(memory_space=pltpu.SMEM)] * 2 + [pl.BlockSpec(memory_space=pl.ANY)] * 3,
        out_specs=pl.BlockSpec(memory_space=pl.ANY),
        scratch_shapes=[
            pltpu.VMEM((rows, features), jnp.bfloat16),
            pltpu.VMEM((stretches, rows, width), jnp.bfloat16),
            pltpu.VMEM((heads, tokens, size), jnp.bfloat16),
            pltpu.VMEM((heads, stretches, rows, size), jnp.bfloat16),
            pltpu.VMEM((stretches, rows, tokens), jnp.bfloat16),
            pltpu.VMEM((2, maps, heads, size, size), jnp.bfloat16),
            pltpu.VMEM((2, modulation.shape[1], 1, width), jnp.float32),
            pltpu.VMEM((2, partners, 8, tokens), jnp.float32),
            dma((stretches,)), dma((stretches,)), dma((stretches,)), dma((stretches,)),
            dma, dma, dma, dma((2,)),
            dma((heads,)), dma((heads,)), dma((heads,)), dma((heads,)), dma((heads,)),
            dma((2, partners)), dma((2, partners)),
            dma((heads, stretches)), dma((heads, stretches)), dma((heads,)),
        ],
        compiler_params=pltpu.CompilerParams(
            collective_id=0, has_side_effects=True, vmem_limit_bytes=56 * 2**20
        ),
        cost_estimate=pl.CostEstimate(flops=flops, bytes_accessed=4 * 2**20, transcendentals=0),
    )(tile_mask, window, latent, head_weights, jnp.swapaxes(modulation, 0, 1))


def solution(mesh):
    sizes = dict(mesh.shape)

    def shards(latent, head_weights, *rest):
        pairs = sizes["section"] == 2 and sizes["groups"] == 2 and head_weights.shape[1] == 4
        even = head_weights.shape[2] % sizes["tm"] == 0
        chosen = gathered_shards if pairs and even else ring_shards
        return chosen(latent, head_weights, *rest)

    return jax.shard_map(
        shards,
        mesh=mesh,
        in_specs=(
            P(("groups", "section"), "tm", "head"),
            P("section", None, "head", None, None),
            P("section", None, "head"),
            P(("groups", "tm"), None, None),
            P("groups"),
        ),
        out_specs=P(("groups", "section"), "tm", "head"),
        check_vma=False,
    )
```

```python
import functools
import math

import jax
import jax.numpy as jnp
from jax import lax
from jax.experimental import pallas as pl
from jax.experimental.pallas import tpu as pltpu
from jax.sharding import PartitionSpec as P

D = 5120


epsilon = 1e-06
MESH_IDS = pl.DeviceIdType.MESH


def from_behind(block, axis, distance):
    devices = range(lax.axis_size(axis))
    route = [(i - distance, i) for i in devices if i - distance in devices]
    return lax.ppermute(block, axis, route)


def passed_along(block, axis, distance):
    devices = range(lax.axis_size(axis))
    route = [((i - distance) % len(devices), i) for i in devices]
    return lax.ppermute(block, axis, route)


def ring_shards(latent, head_weights, modulation, tile_mask, window):
    section_count = lax.axis_size("section")
    my_section = lax.axis_index("section")
    my_stretch = lax.axis_index("tm")
    row_count = latent.shape[1]
    feature_count = latent.shape[2]
    weights = head_weights[0]
    head_count = weights.shape[1]
    head_size = weights.shape[2]
    modulate = modulation[0]
    tile_marks = tile_mask[0]
    tile_count = tile_marks.shape[0]
    span_count = tile_marks.shape[1] // tile_count
    tile_rows = row_count // tile_count
    scale_factor = 1.0 / math.sqrt(head_size)
    expanded = jnp.repeat(jnp.repeat(tile_marks, tile_rows, axis=0), tile_rows, axis=1) == 1
    query_tile = jnp.arange(row_count) // tile_rows
    key_index = jnp.arange(span_count * row_count)
    key_dist = span_count - 1 - key_index // row_count
    key_tile = key_index % row_count // tile_rows
    own_tile = (key_dist == 0)[None, :] & (query_tile[:, None] == key_tile[None, :])
    fixed_mask = expanded | own_tile
    reachable = my_stretch - key_dist >= 0

    def tick_body(tick_index, current):
        clip_index = (my_section - tick_index) % section_count
        active = tick_index == my_section + (section_count - clip_index) % section_count
        win_len = window[clip_index]
        allowed = fixed_mask & (reachable & (key_dist < win_len))[None, :]
        values = current.astype(jnp.float32)
        square_sum = lax.psum(jnp.sum(values * values, axis=-1), "head")
        mean_sq = (square_sum / D)[:, None]
        normed = (values * lax.rsqrt(mean_sq + epsilon) * (1.0 + modulate[1]) + modulate[0]).astype(
            jnp.bfloat16
        )
        heads_in = normed.reshape(row_count, head_count, head_size)
        projected = jnp.einsum(
            "rhd,mhde->mrhe", heads_in, weights[:3], preferred_element_type=jnp.float32
        ).astype(jnp.bfloat16)
        key_value = projected[1:].reshape(2, row_count, feature_count)
        earlier = []
        passed = key_value
        for offset in range(1, span_count):
            passed = from_behind(passed, "tm", 1)
            earlier.append(passed)
        window_keys = jnp.concatenate(earlier[::-1] + [key_value], axis=1)
        window_keys = window_keys.reshape(2, span_count * row_count, head_count, head_size)
        scores = (
            jnp.einsum(
                "qhd,khd->hqk", projected[0], window_keys[0], preferred_element_type=jnp.float32
            )
            * scale_factor
        )
        scores = jnp.where(allowed[None], scores, -1e30)
        row_peak = jnp.max(scores, axis=-1, keepdims=True)
        exponentials = jnp.exp(scores - row_peak)
        attn_probs = (exponentials / jnp.sum(exponentials, axis=-1, keepdims=True)).astype(
            jnp.bfloat16
        )
        attended = jnp.einsum(
            "hqk,khd->qhd", attn_probs, window_keys[1], preferred_element_type=jnp.float32
        ).astype(jnp.bfloat16)
        mixed_out = jnp.einsum(
            "qhd,hde->qhe", attended, weights[3], preferred_element_type=jnp.float32
        ).reshape(row_count, feature_count)
        updated = (values + modulate[2] * mixed_out).astype(jnp.bfloat16)
        current = jnp.where(active, updated, current)
        return passed_along(current, "section", 1)

    finished = lax.fori_loop(0, 2 * section_count, tick_body, latent[0])
    return finished[None]


def rollout_kernel(
    stretches, cores,
    marks_ref, window_ref, latent_ref, weights_ref, modulation_ref,
    out_ref,
    mine, xin, xmid, stage, marks, held, mods, squares,
    in_send, in_recv, mark_send, mark_recv, mine_sem, own_sem, mod_sem, modx_sem,
    local_sem, x_send, x_recv, y_send, y_recv,
    sq_send, sq_recv, out_send, out_recv, out_own,
):
    g = lax.axis_index("groups")
    t = lax.axis_index("tm")
    s = lax.axis_index("section")
    h = lax.axis_index("head")
    heads = held.shape[2]
    size = held.shape[3]
    rows = xin.shape[1]
    width = heads * size
    tokens = stretches * rows
    tiles = marks_ref.shape[1]
    columns = marks_ref.shape[2]
    span = columns // tiles
    scale = 1.0 / math.sqrt(size)
    other_s = 1 - s
    other_g = 1 - g

    peers = [
        (dt, dh, lax.rem(t + dt, stretches), lax.rem(h + dh, cores))
        for dt in range(stretches) for dh in range(cores) if (dt, dh) != (0, 0)
    ]

    def lanes(stretch):
        return pl.ds(pl.multiple_of(stretch * width, size), width)

    def remote(src, dst, send, recv, **where):
        return pltpu.make_async_remote_copy(
            src_ref=src, dst_ref=dst, send_sem=send, recv_sem=recv,
            device_id=where, device_id_type=MESH_IDS,
        )

    barrier = pltpu.get_barrier_semaphore()
    for dt, dh, pt, ph in peers:
        pl.semaphore_signal(barrier, inc=1, device_id={"tm": pt, "head": ph}, device_id_type=MESH_IDS)
    pl.semaphore_signal(barrier, inc=1, device_id={"section": other_s}, device_id_type=MESH_IDS)
    pl.semaphore_signal(barrier, inc=1, device_id={"groups": other_g}, device_id_type=MESH_IDS)

    mine_copy = pltpu.make_async_copy(latent_ref.at[0], mine, mine_sem)
    mine_copy.start()
    own_copy = pltpu.make_async_copy(latent_ref.at[0, :, lanes(t)], xin.at[t], own_sem)
    own_copy.start()
    mod_copy = pltpu.make_async_copy(modulation_ref.at[:, :, lanes(t)], mods.at[s], mod_sem)
    mod_copy.start()
    local = []
    for j in range(heads):
        copy = pltpu.make_async_copy(
            weights_ref.at[0, :, t * heads + j], held.at[s, :, j], local_sem.at[j]
        )
        copy.start()
        local.append(copy)

    row = lax.broadcasted_iota(jnp.int32, (rows, tokens), 0)
    key = lax.broadcasted_iota(jnp.int32, (rows, tokens), 1)
    tile_rows = rows // tiles
    row_tile = row // tile_rows
    key_tile = key % rows // tile_rows
    distance = t - key // rows
    column = (span - 1 - distance) * tiles + key_tile
    marked = jnp.zeros((rows, tokens), jnp.int32)
    for a in range(tiles):
        for c in range(columns):
            marked = jnp.where((row_tile == a) & (column == c), marks_ref[0, a, c], marked)
    own_tile = (distance == 0) & (row_tile == key_tile)
    seen = (distance >= 0) & (distance < window_ref[s]) & (own_tile | (marked == 1))
    marks[t] = jnp.where(seen, 1.0, 0.0).astype(jnp.bfloat16)

    slot = t * cores + h

    def square_copies(layer):
        return [
            remote(
                squares.at[layer, slot], squares.at[layer, slot],
                sq_send.at[layer, dt * cores + dh], sq_recv.at[layer, dt * cores + dh],
                tm=pt, head=ph,
            )
            for dt, dh, pt, ph in peers
        ]

    def put_squares(layer, total):
        turned = total.T
        squares[layer, slot] = jnp.sum(turned.reshape(size // 8, 8, tokens), axis=0)

    mine_copy.wait()
    total = jnp.zeros((rows, size), jnp.float32)
    for j in range(stretches * heads):
        values = mine[:, j * size : (j + 1) * size].astype(jnp.float32)
        total += values * values
    put_squares(0, jnp.concatenate([total] * stretches, axis=0))

    pl.semaphore_wait(barrier, len(peers) + 2)

    half = pl.ds(2 * g, 2)
    other_half = pl.ds(2 * other_g, 2)
    mod_remote = remote(
        modulation_ref.at[:, :, lanes(t)], mods.at[s], modx_sem.at[0], modx_sem.at[1], section=other_s
    )
    x_copies = [
        remote(
            weights_ref.at[0, half, t * heads + j], held.at[s, half, j],
            x_send.at[j], x_recv.at[j], section=other_s,
        )
        for j in range(heads)
    ]
    y_copies = [
        remote(
            held.at[other_s, half, j], held.at[other_s, half, j],
            y_send.at[j], y_recv.at[j], groups=other_g,
        )
        for j in range(heads)
    ]
    in_copies, mark_copies = [], []
    for dt in range(1, stretches):
        pt = lax.rem(t + dt, stretches)
        in_copies.append(
            remote(latent_ref.at[0, :, lanes(pt)], xin.at[t], in_send.at[dt], in_recv.at[dt], tm=pt)
        )
        mark_copies.append(
            remote(marks.at[t], marks.at[t], mark_send.at[dt], mark_recv.at[dt], tm=pt)
        )
    first_squares = square_copies(0)
    for copy in x_copies[:2] + in_copies + first_squares + x_copies[2:] + [mod_remote]:
        copy.start()
    for copy in mark_copies:
        copy.start()

    def forward(j):
        remote(
            weights_ref.at[0, half, t * heads + j], held.at[other_s, half, j],
            x_send.at[j], x_recv.at[j], section=other_s,
        ).wait_recv()
        y_copies[j].start()

    def wait_forwarded(j):
        remote(
            held.at[other_s, half, j], held.at[other_s, other_half, j],
            y_send.at[j], y_recv.at[j], groups=other_g,
        ).wait_recv()

    def row_scale(layer):
        for dt, dh, pt, ph in peers:
            st = lax.rem(t - dt + stretches, stretches)
            sh = lax.rem(h - dh + cores, cores)
            source = st * cores + sh
            remote(
                squares.at[layer, slot], squares.at[layer, source],
                sq_send.at[layer, dt * cores + dh], sq_recv.at[layer, dt * cores + dh],
                tm=pt, head=ph,
            ).wait_recv()
        if layer == 0:
            stretch = lax.broadcasted_iota(jnp.int32, (8, tokens), 1) // rows
            total = jnp.zeros((8, tokens), jnp.float32)
            for source in range(stretches * cores):
                total += jnp.where(stretch == source // cores, squares[0, source], 0.0)
        else:
            total = jnp.sum(squares[layer], axis=0)
        total = jnp.sum(total, axis=0, keepdims=True)
        inverse = lax.rsqrt(total / D + epsilon)
        return jnp.broadcast_to(inverse, (size, tokens)).T

    def block_of(ref, j):
        return ref[:, :, j * size : (j + 1) * size].reshape(tokens, size)

    def some_heads(layer, numbers, inputs, inverse, allowed):
        modulate = [mods[layer, :, 0, j * size : (j + 1) * size] for j in numbers]
        normed = [
            (x * inverse * (1.0 + m[1:2]) + m[0:1]).astype(jnp.bfloat16)
            for x, m in zip(inputs, modulate)
        ]
        q, k, v = (
            [
                jnp.dot(n, held[layer, m, j], preferred_element_type=jnp.float32).astype(jnp.bfloat16)
                for j, n in zip(numbers, normed)
            ]
            for m in range(3)
        )
        scores = [
            lax.dot_general(a, b, (((1,), (1,)), ((), ())), preferred_element_type=jnp.float32) * scale
            for a, b in zip(q, k)
        ]
        scores = [jnp.where(allowed, x, -1e30) for x in scores]
        weight = [jnp.exp(x - jnp.max(x, axis=-1, keepdims=True)) for x in scores]
        probs = [(x / jnp.sum(x, axis=-1, keepdims=True)).astype(jnp.bfloat16) for x in weight]
        attended = [
            jnp.dot(p, b, preferred_element_type=jnp.float32).astype(jnp.bfloat16)
            for p, b in zip(probs, v)
        ]
        mixed = [
            jnp.dot(a, held[layer, 3, j], preferred_element_type=jnp.float32)
            for j, a in zip(numbers, attended)
        ]
        return [
            (x + m[2:3] * y).astype(jnp.bfloat16) for x, m, y in zip(inputs, modulate, mixed)
        ]

    def ahead(j):
        if j < heads:
            forward(j)

    ahead(0)
    ahead(1)
    own_copy.wait()
    for dt in range(1, stretches):
        st = lax.rem(t - dt + stretches, stretches)
        remote(
            latent_ref.at[0, :, lanes(t)], xin.at[st], in_send.at[dt], in_recv.at[dt], tm=st
        ).wait_recv()
    ahead(2)

    for dt in range(1, stretches):
        st = lax.rem(t - dt + stretches, stretches)
        remote(marks.at[t], marks.at[st], mark_send.at[dt], mark_recv.at[dt], tm=st).wait_recv()
    mod_copy.wait()
    remote(
        modulation_ref.at[:, :, lanes(t)], mods.at[other_s], modx_sem.at[0], modx_sem.at[1], section=other_s
    ).wait_recv()
    allowed = marks[...].reshape(tokens, tokens).astype(jnp.float32) > 0.5

    inverse = row_scale(0)
    ahead(3)
    total = jnp.zeros((tokens, size), jnp.float32)
    for group in (range(heads // 2), range(heads // 2, heads)):
        for j in group:
            ahead(j + 4)

        @pl.when(s == 0)
        def _():
            for j in group:
                local[j].wait()

        @pl.when(s == 1)
        def _():
            for j in group:
                wait_forwarded(j)

        inputs = [block_of(xin, j).astype(jnp.float32) for j in group]
        for j, result in zip(group, some_heads(0, group, inputs, inverse, allowed)):
            xmid[j] = result
            rounded = result.astype(jnp.float32)
            total += rounded * rounded
    put_squares(1, total)
    for copy in square_copies(1):
        copy.start()

    @pl.when(s == 0)
    def _():
        for j in range(heads):
            wait_forwarded(j)

    @pl.when(s == 1)
    def _():
        for j in range(heads):
            local[j].wait()

    inverse = row_scale(1)
    numbers = list(range(heads))
    inputs = [xmid[j].astype(jnp.float32) for j in numbers]
    for j, result in enumerate(some_heads(1, numbers, inputs, inverse, allowed)):
        stage[:, :, j * size : (j + 1) * size] = result.reshape(stretches, rows, size)
    finals = []
    for dt in range(1, stretches):
        pt = lax.rem(t + dt, stretches)
        copy = remote(
            stage.at[pt], out_ref.at[0, :, lanes(t)], out_send.at[0, dt], out_recv.at[0, dt], tm=pt
        )
        copy.start()
        finals.append(copy)
    last = pltpu.make_async_copy(stage.at[t], out_ref.at[0, :, lanes(t)], out_own.at[0])
    last.start()

    for copy in in_copies + mark_copies + [mod_remote] + x_copies + y_copies:
        copy.wait_send()
    for layer in range(2):
        for copy in square_copies(layer):
            copy.wait_send()
    for dt in range(1, stretches):
        st = lax.rem(t - dt + stretches, stretches)
        finals[dt - 1].wait_send()
        remote(
            stage.at[t], out_ref.at[0, :, lanes(st)], out_send.at[0, dt], out_recv.at[0, dt], tm=st
        ).wait_recv()
    last.wait()


def gathered_shards(latent, head_weights, modulation, tile_mask, window):
    stretches = lax.axis_size("tm")
    cores = lax.axis_size("head")
    rows, features = latent.shape[1:]
    maps, head_count, size = head_weights.shape[1:4]
    heads = head_count // stretches
    width = heads * size
    tokens = stretches * rows
    partners = stretches * cores
    dma = pltpu.SemaphoreType.DMA
    flops = 2 * heads * 6 * 2 * tokens * size * size
    return pl.pallas_call(
        functools.partial(rollout_kernel, stretches, cores),
        out_shape=jax.ShapeDtypeStruct(latent.shape, latent.dtype),
        in_specs=[pl.BlockSpec(memory_space=pltpu.SMEM)] * 2 + [pl.BlockSpec(memory_space=pl.ANY)] * 3,
        out_specs=pl.BlockSpec(memory_space=pl.ANY),
        scratch_shapes=[
            pltpu.VMEM((rows, features), jnp.bfloat16),
            pltpu.VMEM((stretches, rows, width), jnp.bfloat16),
            pltpu.VMEM((heads, tokens, size), jnp.bfloat16),
            pltpu.VMEM((stretches, rows, width), jnp.bfloat16),
            pltpu.VMEM((stretches, rows, tokens), jnp.bfloat16),
            pltpu.VMEM((2, maps, heads, size, size), jnp.bfloat16),
            pltpu.VMEM((2, modulation.shape[1], 1, width), jnp.float32),
            pltpu.VMEM((2, partners, 8, tokens), jnp.float32),
            dma((stretches,)), dma((stretches,)), dma((stretches,)), dma((stretches,)),
            dma, dma, dma, dma((2,)),
            dma((heads,)), dma((heads,)), dma((heads,)), dma((heads,)), dma((heads,)),
            dma((2, partners)), dma((2, partners)),
            dma((heads, stretches)), dma((heads, stretches)), dma((heads,)),
        ],
        compiler_params=pltpu.CompilerParams(
            collective_id=0, has_side_effects=True, vmem_limit_bytes=56 * 2**20
        ),
        cost_estimate=pl.CostEstimate(flops=flops, bytes_accessed=4 * 2**20, transcendentals=0),
    )(tile_mask, window, latent, head_weights, jnp.swapaxes(modulation, 0, 1))


def solution(mesh):
    sizes = dict(mesh.shape)

    def shards(latent, head_weights, *rest):
        pairs = sizes["section"] == 2 and sizes["groups"] == 2 and head_weights.shape[1] == 4
        even = head_weights.shape[2] % sizes["tm"] == 0
        chosen = gathered_shards if pairs and even else ring_shards
        return chosen(latent, head_weights, *rest)

    return jax.shard_map(
        shards,
        mesh=mesh,
        in_specs=(
            P(("groups", "section"), "tm", "head"),
            P("section", None, "head", None, None),
            P("section", None, "head"),
            P(("groups", "tm"), None, None),
            P("groups"),
        ),
        out_specs=P(("groups", "section"), "tm", "head"),
        check_vma=False,
    )
```

```python
import functools
import math

import jax
import jax.numpy as jnp
from jax import lax
from jax.experimental import pallas as pl
from jax.experimental.pallas import tpu as pltpu
from jax.sharding import PartitionSpec as P

D = 5120


epsilon = 1e-06
MESH_IDS = pl.DeviceIdType.MESH


def from_behind(block, axis, distance):
    devices = range(lax.axis_size(axis))
    route = [(i - distance, i) for i in devices if i - distance in devices]
    return lax.ppermute(block, axis, route)


def passed_along(block, axis, distance):
    devices = range(lax.axis_size(axis))
    route = [((i - distance) % len(devices), i) for i in devices]
    return lax.ppermute(block, axis, route)


def ring_shards(latent, head_weights, modulation, tile_mask, window):
    section_count = lax.axis_size("section")
    my_section = lax.axis_index("section")
    my_stretch = lax.axis_index("tm")
    row_count = latent.shape[1]
    feature_count = latent.shape[2]
    weights = head_weights[0]
    head_count = weights.shape[1]
    head_size = weights.shape[2]
    modulate = modulation[0]
    tile_marks = tile_mask[0]
    tile_count = tile_marks.shape[0]
    span_count = tile_marks.shape[1] // tile_count
    tile_rows = row_count // tile_count
    scale_factor = 1.0 / math.sqrt(head_size)
    expanded = jnp.repeat(jnp.repeat(tile_marks, tile_rows, axis=0), tile_rows, axis=1) == 1
    query_tile = jnp.arange(row_count) // tile_rows
    key_index = jnp.arange(span_count * row_count)
    key_dist = span_count - 1 - key_index // row_count
    key_tile = key_index % row_count // tile_rows
    own_tile = (key_dist == 0)[None, :] & (query_tile[:, None] == key_tile[None, :])
    fixed_mask = expanded | own_tile
    reachable = my_stretch - key_dist >= 0

    def tick_body(tick_index, current):
        clip_index = (my_section - tick_index) % section_count
        active = tick_index == my_section + (section_count - clip_index) % section_count
        win_len = window[clip_index]
        allowed = fixed_mask & (reachable & (key_dist < win_len))[None, :]
        values = current.astype(jnp.float32)
        square_sum = lax.psum(jnp.sum(values * values, axis=-1), "head")
        mean_sq = (square_sum / D)[:, None]
        normed = (values * lax.rsqrt(mean_sq + epsilon) * (1.0 + modulate[1]) + modulate[0]).astype(
            jnp.bfloat16
        )
        heads_in = normed.reshape(row_count, head_count, head_size)
        projected = jnp.einsum(
            "rhd,mhde->mrhe", heads_in, weights[:3], preferred_element_type=jnp.float32
        ).astype(jnp.bfloat16)
        key_value = projected[1:].reshape(2, row_count, feature_count)
        earlier = []
        passed = key_value
        for offset in range(1, span_count):
            passed = from_behind(passed, "tm", 1)
            earlier.append(passed)
        window_keys = jnp.concatenate(earlier[::-1] + [key_value], axis=1)
        window_keys = window_keys.reshape(2, span_count * row_count, head_count, head_size)
        scores = (
            jnp.einsum(
                "qhd,khd->hqk", projected[0], window_keys[0], preferred_element_type=jnp.float32
            )
            * scale_factor
        )
        scores = jnp.where(allowed[None], scores, -1e30)
        row_peak = jnp.max(scores, axis=-1, keepdims=True)
        exponentials = jnp.exp(scores - row_peak)
        attn_probs = (exponentials / jnp.sum(exponentials, axis=-1, keepdims=True)).astype(
            jnp.bfloat16
        )
        attended = jnp.einsum(
            "hqk,khd->qhd", attn_probs, window_keys[1], preferred_element_type=jnp.float32
        ).astype(jnp.bfloat16)
        mixed_out = jnp.einsum(
            "qhd,hde->qhe", attended, weights[3], preferred_element_type=jnp.float32
        ).reshape(row_count, feature_count)
        updated = (values + modulate[2] * mixed_out).astype(jnp.bfloat16)
        current = jnp.where(active, updated, current)
        return passed_along(current, "section", 1)

    finished = lax.fori_loop(0, 2 * section_count, tick_body, latent[0])
    return finished[None]


def rollout_kernel(
    stretches, cores,
    marks_ref, window_ref, latent_ref, weights_ref, modulation_ref,
    out_ref,
    mine, xin, xmid, stage, marks, held, mods, squares,
    in_send, in_recv, mark_send, mark_recv, mine_sem, own_sem, mod_sem, modx_sem,
    local_sem, x_send, x_recv, y_send, y_recv,
    sq_send, sq_recv, out_send, out_recv, out_own,
):
    g = lax.axis_index("groups")
    t = lax.axis_index("tm")
    s = lax.axis_index("section")
    h = lax.axis_index("head")
    heads = held.shape[2]
    size = held.shape[3]
    rows = xin.shape[1]
    width = heads * size
    tokens = stretches * rows
    tiles = marks_ref.shape[1]
    columns = marks_ref.shape[2]
    span = columns // tiles
    scale = 1.0 / math.sqrt(size)
    other_s = 1 - s
    other_g = 1 - g

    peers = [
        (dt, dh, lax.rem(t + dt, stretches), lax.rem(h + dh, cores))
        for dt in range(stretches) for dh in range(cores) if (dt, dh) != (0, 0)
    ]

    def lanes(stretch):
        return pl.ds(pl.multiple_of(stretch * width, size), width)

    def remote(src, dst, send, recv, **where):
        return pltpu.make_async_remote_copy(
            src_ref=src, dst_ref=dst, send_sem=send, recv_sem=recv,
            device_id=where, device_id_type=MESH_IDS,
        )

    barrier = pltpu.get_barrier_semaphore()
    for dt, dh, pt, ph in peers:
        pl.semaphore_signal(barrier, inc=1, device_id={"tm": pt, "head": ph}, device_id_type=MESH_IDS)
    pl.semaphore_signal(barrier, inc=1, device_id={"section": other_s}, device_id_type=MESH_IDS)
    pl.semaphore_signal(barrier, inc=1, device_id={"groups": other_g}, device_id_type=MESH_IDS)

    mine_copy = pltpu.make_async_copy(latent_ref.at[0], mine, mine_sem)
    mine_copy.start()
    own_copy = pltpu.make_async_copy(latent_ref.at[0, :, lanes(t)], xin.at[t], own_sem)
    own_copy.start()
    mod_copy = pltpu.make_async_copy(modulation_ref.at[:, :, lanes(t)], mods.at[s], mod_sem)
    mod_copy.start()
    local = []
    for j in range(heads):
        copy = pltpu.make_async_copy(
            weights_ref.at[0, :, t * heads + j], held.at[s, :, j], local_sem.at[j]
        )
        copy.start()
        local.append(copy)

    row = lax.broadcasted_iota(jnp.int32, (rows, tokens), 0)
    key = lax.broadcasted_iota(jnp.int32, (rows, tokens), 1)
    tile_rows = rows // tiles
    row_tile = row // tile_rows
    key_tile = key % rows // tile_rows
    distance = t - key // rows
    column = (span - 1 - distance) * tiles + key_tile
    marked = jnp.zeros((rows, tokens), jnp.int32)
    for a in range(tiles):
        for c in range(columns):
            marked = jnp.where((row_tile == a) & (column == c), marks_ref[0, a, c], marked)
    own_tile = (distance == 0) & (row_tile == key_tile)
    seen = (distance >= 0) & (distance < window_ref[s]) & (own_tile | (marked == 1))
    marks[t] = jnp.where(seen, 1.0, 0.0).astype(jnp.bfloat16)

    slot = t * cores + h

    def square_copies(layer):
        return [
            remote(
                squares.at[layer, slot], squares.at[layer, slot],
                sq_send.at[layer, dt * cores + dh], sq_recv.at[layer, dt * cores + dh],
                tm=pt, head=ph,
            )
            for dt, dh, pt, ph in peers
        ]

    def put_squares(layer, total):
        turned = total.T
        squares[layer, slot] = jnp.sum(turned.reshape(size // 8, 8, tokens), axis=0)

    mine_copy.wait()
    total = jnp.zeros((rows, size), jnp.float32)
    for j in range(stretches * heads):
        values = mine[:, j * size : (j + 1) * size].astype(jnp.float32)
        total += values * values
    put_squares(0, jnp.concatenate([total] * stretches, axis=0))

    pl.semaphore_wait(barrier, len(peers) + 2)

    half = pl.ds(2 * g, 2)
    other_half = pl.ds(2 * other_g, 2)
    mod_remote = remote(
        modulation_ref.at[:, :, lanes(t)], mods.at[s], modx_sem.at[0], modx_sem.at[1], section=other_s
    )
    x_copies = [
        remote(
            weights_ref.at[0, half, t * heads + j], held.at[s, half, j],
            x_send.at[j], x_recv.at[j], section=other_s,
        )
        for j in range(heads)
    ]
    y_copies = [
        remote(
            held.at[other_s, half, j], held.at[other_s, half, j],
            y_send.at[j], y_recv.at[j], groups=other_g,
        )
        for j in range(heads)
    ]
    in_copies, mark_copies = [], []
    for dt in range(1, stretches):
        pt = lax.rem(t + dt, stretches)
        in_copies.append(
            remote(latent_ref.at[0, :, lanes(pt)], xin.at[t], in_send.at[dt], in_recv.at[dt], tm=pt)
        )
        mark_copies.append(
            remote(marks.at[t], marks.at[t], mark_send.at[dt], mark_recv.at[dt], tm=pt)
        )
    first_squares = square_copies(0)
    for copy in x_copies + in_copies[::-1] + first_squares[::-1] + [mod_remote]:
        copy.start()
    for copy in mark_copies:
        copy.start()

    def forward(j):
        remote(
            weights_ref.at[0, half, t * heads + j], held.at[other_s, half, j],
            x_send.at[j], x_recv.at[j], section=other_s,
        ).wait_recv()
        y_copies[j].start()

    def wait_forwarded(j):
        remote(
            held.at[other_s, half, j], held.at[other_s, other_half, j],
            y_send.at[j], y_recv.at[j], groups=other_g,
        ).wait_recv()

    def row_scale(layer):
        for dt, dh, pt, ph in peers:
            st = lax.rem(t - dt + stretches, stretches)
            sh = lax.rem(h - dh + cores, cores)
            source = st * cores + sh
            remote(
                squares.at[layer, slot], squares.at[layer, source],
                sq_send.at[layer, dt * cores + dh], sq_recv.at[layer, dt * cores + dh],
                tm=pt, head=ph,
            ).wait_recv()
        if layer == 0:
            stretch = lax.broadcasted_iota(jnp.int32, (8, tokens), 1) // rows
            total = jnp.zeros((8, tokens), jnp.float32)
            for source in range(stretches * cores):
                total += jnp.where(stretch == source // cores, squares[0, source], 0.0)
        else:
            total = jnp.sum(squares[layer], axis=0)
        total = jnp.sum(total, axis=0, keepdims=True)
        inverse = lax.rsqrt(total / D + epsilon)
        return jnp.broadcast_to(inverse, (size, tokens)).T

    def block_of(ref, j):
        return ref[:, :, j * size : (j + 1) * size].reshape(tokens, size)

    def some_heads(layer, numbers, inputs, inverse, allowed):
        modulate = [mods[layer, :, 0, j * size : (j + 1) * size] for j in numbers]
        normed = [
            (x * inverse * (1.0 + m[1:2]) + m[0:1]).astype(jnp.bfloat16)
            for x, m in zip(inputs, modulate)
        ]
        q, k, v = (
            [
                jnp.dot(n, held[layer, m, j], preferred_element_type=jnp.float32).astype(jnp.bfloat16)
                for j, n in zip(numbers, normed)
            ]
            for m in range(3)
        )
        scores = [
            lax.dot_general(a, b, (((1,), (1,)), ((), ())), preferred_element_type=jnp.float32) * scale
            for a, b in zip(q, k)
        ]
        scores = [jnp.where(allowed, x, -1e30) for x in scores]
        weight = [jnp.exp(x - jnp.max(x, axis=-1, keepdims=True)) for x in scores]
        probs = [(x / jnp.sum(x, axis=-1, keepdims=True)).astype(jnp.bfloat16) for x in weight]
        attended = [
            jnp.dot(p, b, preferred_element_type=jnp.float32).astype(jnp.bfloat16)
            for p, b in zip(probs, v)
        ]
        mixed = [
            jnp.dot(a, held[layer, 3, j], preferred_element_type=jnp.float32)
            for j, a in zip(numbers, attended)
        ]
        return [
            (x + m[2:3] * y).astype(jnp.bfloat16) for x, m, y in zip(inputs, modulate, mixed)
        ]

    def ahead(j):
        if j < heads:
            forward(j)

    ahead(0)
    ahead(1)
    own_copy.wait()
    for dt in range(1, stretches):
        st = lax.rem(t - dt + stretches, stretches)
        remote(
            latent_ref.at[0, :, lanes(t)], xin.at[st], in_send.at[dt], in_recv.at[dt], tm=st
        ).wait_recv()
    ahead(2)
    ahead(3)
    for j in range(4, heads):
        ahead(j)

    for dt in range(1, stretches):
        st = lax.rem(t - dt + stretches, stretches)
        remote(marks.at[t], marks.at[st], mark_send.at[dt], mark_recv.at[dt], tm=st).wait_recv()
    mod_copy.wait()
    remote(
        modulation_ref.at[:, :, lanes(t)], mods.at[other_s], modx_sem.at[0], modx_sem.at[1], section=other_s
    ).wait_recv()
    allowed = marks[...].reshape(tokens, tokens).astype(jnp.float32) > 0.5

    inverse = row_scale(0)
    total = jnp.zeros((tokens, size), jnp.float32)
    for group in (range(heads // 2), range(heads // 2, heads)):
        @pl.when(s == 0)
        def _():
            for j in group:
                local[j].wait()

        @pl.when(s == 1)
        def _():
            for j in group:
                wait_forwarded(j)

        inputs = [block_of(xin, j).astype(jnp.float32) for j in group]
        for j, result in zip(group, some_heads(0, group, inputs, inverse, allowed)):
            xmid[j] = result
            rounded = result.astype(jnp.float32)
            total += rounded * rounded
    put_squares(1, total)
    for copy in square_copies(1)[::-1]:
        copy.start()

    @pl.when(s == 0)
    def _():
        for j in range(heads):
            wait_forwarded(j)

    @pl.when(s == 1)
    def _():
        for j in range(heads):
            local[j].wait()

    inverse = row_scale(1)
    numbers = list(range(heads))
    inputs = [xmid[j].astype(jnp.float32) for j in numbers]
    for j, result in enumerate(some_heads(1, numbers, inputs, inverse, allowed)):
        stage[:, :, j * size : (j + 1) * size] = result.reshape(stretches, rows, size)
    finals = []
    for dt in range(1, stretches):
        pt = lax.rem(t + dt, stretches)
        copy = remote(
            stage.at[pt], out_ref.at[0, :, lanes(t)], out_send.at[0, dt], out_recv.at[0, dt], tm=pt
        )
        copy.start()
        finals.append(copy)
    last = pltpu.make_async_copy(stage.at[t], out_ref.at[0, :, lanes(t)], out_own.at[0])
    last.start()

    for copy in in_copies + mark_copies + [mod_remote] + x_copies + y_copies:
        copy.wait_send()
    for layer in range(2):
        for copy in square_copies(layer):
            copy.wait_send()
    for dt in range(1, stretches):
        st = lax.rem(t - dt + stretches, stretches)
        finals[dt - 1].wait_send()
        remote(
            stage.at[t], out_ref.at[0, :, lanes(st)], out_send.at[0, dt], out_recv.at[0, dt], tm=st
        ).wait_recv()
    last.wait()


def gathered_shards(latent, head_weights, modulation, tile_mask, window):
    stretches = lax.axis_size("tm")
    cores = lax.axis_size("head")
    rows, features = latent.shape[1:]
    maps, head_count, size = head_weights.shape[1:4]
    heads = head_count // stretches
    width = heads * size
    tokens = stretches * rows
    partners = stretches * cores
    dma = pltpu.SemaphoreType.DMA
    flops = 2 * heads * 6 * 2 * tokens * size * size
    return pl.pallas_call(
        functools.partial(rollout_kernel, stretches, cores),
        out_shape=jax.ShapeDtypeStruct(latent.shape, latent.dtype),
        in_specs=[pl.BlockSpec(memory_space=pltpu.SMEM)] * 2 + [pl.BlockSpec(memory_space=pl.ANY)] * 3,
        out_specs=pl.BlockSpec(memory_space=pl.ANY),
        scratch_shapes=[
            pltpu.VMEM((rows, features), jnp.bfloat16),
            pltpu.VMEM((stretches, rows, width), jnp.bfloat16),
            pltpu.VMEM((heads, tokens, size), jnp.bfloat16),
            pltpu.VMEM((stretches, rows, width), jnp.bfloat16),
            pltpu.VMEM((stretches, rows, tokens), jnp.bfloat16),
            pltpu.VMEM((2, maps, heads, size, size), jnp.bfloat16),
            pltpu.VMEM((2, modulation.shape[1], 1, width), jnp.float32),
            pltpu.VMEM((2, partners, 8, tokens), jnp.float32),
            dma((stretches,)), dma((stretches,)), dma((stretches,)), dma((stretches,)),
            dma, dma, dma, dma((2,)),
            dma((heads,)), dma((heads,)), dma((heads,)), dma((heads,)), dma((heads,)),
            dma((2, partners)), dma((2, partners)),
            dma((heads, stretches)), dma((heads, stretches)), dma((heads,)),
        ],
        compiler_params=pltpu.CompilerParams(
            collective_id=0, has_side_effects=True, vmem_limit_bytes=56 * 2**20
        ),
        cost_estimate=pl.CostEstimate(flops=flops, bytes_accessed=4 * 2**20, transcendentals=0),
    )(tile_mask, window, latent, head_weights, jnp.swapaxes(modulation, 0, 1))


def solution(mesh):
    sizes = dict(mesh.shape)

    def shards(latent, head_weights, *rest):
        pairs = sizes["section"] == 2 and sizes["groups"] == 2 and head_weights.shape[1] == 4
        even = head_weights.shape[2] % sizes["tm"] == 0
        chosen = gathered_shards if pairs and even else ring_shards
        return chosen(latent, head_weights, *rest)

    return jax.shard_map(
        shards,
        mesh=mesh,
        in_specs=(
            P(("groups", "section"), "tm", "head"),
            P("section", None, "head", None, None),
            P("section", None, "head"),
            P(("groups", "tm"), None, None),
            P("groups"),
        ),
        out_specs=P(("groups", "section"), "tm", "head"),
        check_vma=False,
    )
```
